256 devices in a mesh: tile: 32 (over y, x, core), pair: 8 (over z).
Axes of the slice: x: 4, y: 4, z: 8, core: 2. Of those that a mesh axis runs over, the one named last changes fastest.
Arguments:
- l_tiles: bfloat16 [768, 32768], P('pair', 'tile'), may hold values from -6 to 6
- nz_lists: int32 [8, 32, 8], P('pair', 'tile'), may hold values from 0 to 9, as said below
- v_slab: bfloat16 [32, 8, 1280, 1280], P('tile', 'pair'), may hold values from -0.046875 to 0.046875
Outputs:
- ladder: float32 [768, 40960], P('pair', 'tile')
The draws below stay inside these ranges and needn't reach their ends.
Inputs may be any that keep to these rules, and one draw needn't show every extreme that they name: Each row nz_lists(b, g, :) names 8 different blocks of the 10 in group g, in increasing order.
All inputs are finite; a program needn't handle non-finite values.
Results may differ from the reference program's by a relative error of at most 0.0003.
Values may be sent and summed in bfloat16 or wider, within the bound.
A program may use at most 64 MiB of HBM per device.

```python
import jax
import jax.numpy as jnp
from jax import lax

B = 128
KB = 10
NZ = 8
P_DEV = 96
NB = 8
ND = 8
NG = 32
NP = 768
W = 1280


def draw_nz_lists(key, part):
    key = jax.random.fold_in(key, 11)
    keys = jax.random.split(key, NB * NG)
    orders = jax.vmap(lambda one_key: jax.random.permutation(one_key, KB))(keys)
    chosen = jnp.sort(orders[:, :NZ], axis=1)
    return chosen.reshape(NB, NG, NZ).astype(jnp.int32)


def block_levels(own_key, dims, cuts, least, high):
    loudness, own = 1.0, jax.random.fold_in(own_key, 6)
    for axis_at, blocks in cuts:
        draws = jnp.exp(jax.random.uniform(jax.random.fold_in(own, axis_at), (blocks,), jnp.float32, least / len(cuts), high / len(cuts)))
        loudness = loudness * jnp.repeat(draws, dims[axis_at] // blocks).reshape([-1 if axis == axis_at else 1 for axis in range(len(dims))])
    return loudness


def gaussian(rng, shape, spread, bound, cuts=(), kind=jnp.bfloat16):
    factor_of = block_levels(rng, shape, cuts, -0.22, 0.18) if cuts else 1.0
    array = jax.random.normal(rng, shape, jnp.float32) * spread * factor_of
    return jnp.minimum(jnp.maximum(array, -bound), bound).astype(kind)


def setup_inputs(seed: int = 0) -> dict:
    splits = jax.random.split(jax.random.key(seed), 4)
    l_tiles = gaussian(splits[0], (NP, NG * NZ * B), 1.0, 6.0, ((0, 8), (1, 32)))
    nz_lists = draw_nz_lists(jax.random.fold_in(splits[3], 71), 0)
    v_slab = gaussian(splits[2], (NG, ND, W, W), ((2 * ND - 1) * NZ * B) ** -0.5, 0.046875, ((0, 32), (1, 8)))
    return dict(l_tiles=l_tiles, nz_lists=nz_lists, v_slab=v_slab)


def expand_rows(tile_rows, list_rows):
    shaped = tile_rows.reshape(NB, P_DEV, NG, NZ, B).astype(jnp.float32)
    onehot = (list_rows[..., None] == jnp.arange(KB, dtype=jnp.int32)).astype(jnp.float32)
    dense_rows = jnp.einsum('bpgeu,bgek->bpgku', shaped, onehot)
    return dense_rows.reshape(NP, NG, W).astype(jnp.bfloat16)


def reference(l_tiles, nz_lists, v_slab):
    dense_rows = expand_rows(l_tiles, nz_lists)
    row_ids = jnp.arange(W)[:, None]
    col_ids = jnp.arange(W)[None, :]
    upper_part = row_ids <= col_ids
    strict = row_ids < col_ids

    def per_group(ladder, group_index):
        own_rows = lax.dynamic_index_in_dim(dense_rows, group_index, 1, keepdims=False)
        group_slab = lax.dynamic_index_in_dim(v_slab, group_index, 0, keepdims=False)
        for offset in range(ND):
            target = (group_index + offset) % NG
            v_block = group_slab[offset]
            if offset == 0:
                direct_block = jnp.where(upper_part, v_block, jnp.zeros_like(v_block))
                mirror_block = jnp.where(strict, v_block, jnp.zeros_like(v_block))
            else:
                direct_block = v_block
                mirror_block = v_block
            far_rows = lax.dynamic_index_in_dim(dense_rows, target, 1, keepdims=False)
            direct = jnp.dot(own_rows, direct_block, preferred_element_type=jnp.float32)
            mirror = lax.dot_general(far_rows, mirror_block, (((1,), (1,)), ((), ())), preferred_element_type=jnp.float32)
            ladder = ladder.at[:, target].add(direct)
            ladder = ladder.at[:, group_index].add(mirror)
        return ladder, None

    ladder, _ = lax.scan(per_group, jnp.zeros((NP, NG, W), jnp.float32), jnp.arange(NG, dtype=jnp.int32))
    return ladder.reshape(NP, NG * W)
```

```python
import functools

import jax
import jax.numpy as jnp
from jax import lax
from jax.experimental import pallas as pl
from jax.experimental.pallas import tpu as pltpu
from jax.sharding import PartitionSpec as P

MESH = pl.DeviceIdType.MESH
B = 128
KB = 10
NZ = 8
P_DEV = 96
W = B * KB
NB = 8
NG = 32
MSG = NZ * P_DEV + 16
CB = 256
HALF = 4 * P_DEV
REL = (4, 3, -3, 2, -2, 1, -1, 0)
SLOT = {rel: slot for slot, rel in enumerate(REL)}
SLOT[-4] = SLOT[4]
QMAX = 32767.0


def encode(values):
    top = jnp.maximum(jnp.max(jnp.abs(values), axis=0, keepdims=True), 1e-30)
    coded = jnp.round(values * (QMAX / top)).astype(jnp.int32).astype(jnp.int16)
    return coded, top * (1.0 / QMAX)


def decode(coded, scale):
    return coded.astype(jnp.int32).astype(jnp.float32) * scale


def columns(j):
    return pl.ds(pl.multiple_of(j * CB, CB), CB)


def kernel(
    nz_ref, l_ref, v_ref, out_ref,
    own, far, dense_own, dense_far, v_dir, v_mir, mirror,
    d_out, d_out_sc, d_in, d_in_sc, r_out, r_out_sc, r_in, r_in_sc,
    v_sem, ag_s, ag_r, far_s, far_r, d_s, d_r, dsc_s, dsc_r, r_s, r_r, rsc_s, rsc_r,
):
    t = lax.axis_index("tile")
    z = lax.axis_index("pair")
    up = (t, lax.rem(z + 1, NB))
    down = (t, lax.rem(z + NB - 1, NB))
    ahead = (lax.rem(t + z, NG), z)
    behind = (lax.rem(t + NG - z, NG), z)
    shifted = z > 0

    loads = [
        pltpu.make_async_copy(v_ref.at[0, 0], v_dir, v_sem.at[0]),
        pltpu.make_async_copy(v_ref.at[0, 0], v_mir, v_sem.at[1]),
    ]
    for load in loads:
        load.start()

    barrier = pltpu.get_barrier_semaphore()
    for device in (up, down):
        pl.semaphore_signal(barrier, inc=1, device_id=device, device_id_type=MESH)

    @pl.when(shifted)
    def _():
        for device in (ahead, behind):
            pl.semaphore_signal(barrier, inc=1, device_id=device, device_id_type=MESH)

    me = SLOT[0]
    for e in range(NZ):
        own[me, e * P_DEV:(e + 1) * P_DEV, :] = l_ref[:, e * B:(e + 1) * B]
    entry = lax.broadcasted_iota(jnp.int32, (16, B), 0)
    listed = jnp.zeros((16, B), jnp.int32)
    for e in range(NZ):
        listed = jnp.where(entry == e, nz_ref[0, 0, e], listed)
    own[me, NZ * P_DEV:, :] = listed.astype(jnp.float32).astype(jnp.bfloat16)

    pl.semaphore_wait(barrier, 2 + 2 * jnp.minimum(z, 1))

    def remote(src, dst, send, recv, device):
        return pltpu.make_async_remote_copy(
            src_ref=src, dst_ref=dst, send_sem=send, recv_sem=recv,
            device_id=device, device_id_type=MESH,
        )

    def gather_copy(rel, step):
        src, dst = SLOT[rel], SLOT[rel - step]
        return remote(own.at[src], own.at[dst], ag_s.at[dst], ag_r.at[dst], up if step == 1 else down)

    def far_copy(slot):
        return remote(far_src(slot), far.at[slot], far_s.at[slot], far_r.at[slot], behind)

    def far_src(slot):
        return own.at[slot]

    def d_copies(slot):
        return (
            remote(d_out.at[slot], d_in.at[slot], d_s.at[slot], d_r.at[slot], ahead),
            remote(d_out_sc.at[slot], d_in_sc.at[slot], dsc_s.at[slot], dsc_r.at[slot], ahead),
        )

    def r_copies(rel, step):
        src, dst = SLOT[rel], SLOT[rel - step]
        lane = 0 if step == 1 else 1
        device = up if step == 1 else down
        return (
            remote(r_out.at[src], r_in.at[lane, dst], r_s.at[src], r_r.at[lane, dst], device),
            remote(r_out_sc.at[src], r_in_sc.at[lane, dst], rsc_s.at[src], rsc_r.at[lane, dst], device),
        )

    def expand(msg, slot, dense):
        lists = msg[slot, NZ * P_DEV:, :].astype(jnp.float32)
        for k in range(KB):
            total = None
            for e in range(max(0, k - KB + NZ), min(NZ - 1, k) + 1):
                hit = jnp.where(lists[e:e + 1, :] == float(k), 1.0, 0.0).astype(jnp.bfloat16)
                term = msg[slot, e * P_DEV:(e + 1) * P_DEV, :] * hit
                total = term if total is None else total + term
            dense[slot * P_DEV:(slot + 1) * P_DEV, k * B:(k + 1) * B] = total

    gather_sends = []

    def gather_start(rel, step):
        copy = gather_copy(rel, step)
        copy.start()
        gather_sends.append(copy)

    def far_start(slot):
        @pl.when(shifted)
        def _():
            far_copy(slot).start()

    gather_start(0, 1)
    gather_start(0, -1)
    far_start(me)
    for load in loads:
        load.wait()

    @pl.when(z == 0)
    def _():
        def mask(i, carry):
            rows = pl.ds(pl.multiple_of(i * B, B), B)
            row_ids = lax.broadcasted_iota(jnp.int32, (B, W), 0) + i * B
            col_ids = lax.broadcasted_iota(jnp.int32, (B, W), 1)
            block = v_dir[rows, :].astype(jnp.float32)
            v_dir[rows, :] = jnp.where(row_ids <= col_ids, block, 0.0).astype(jnp.bfloat16)
            v_mir[rows, :] = jnp.where(row_ids < col_ids, block, 0.0).astype(jnp.bfloat16)
            return carry

        lax.fori_loop(0, KB, mask, 0)

    expand(own, me, dense_own)

    for r in range(1, 5):
        gather_copy(-r + 1, 1).wait_recv()
        if r < 4:
            gather_start(-r, 1)
        far_start(SLOT[-r])
        if r < 4:
            gather_copy(r - 1, -1).wait_recv()
            if r < 3:
                gather_start(r, -1)
            far_start(SLOT[r])
        expand(own, SLOT[-r], dense_own)
        if r < 4:
            expand(own, SLOT[r], dense_own)

    def direct_half(first):
        def block(j, carry):
            part = jnp.dot(
                dense_own[first * P_DEV:first * P_DEV + HALF, :], v_dir[:, columns(j)],
                preferred_element_type=jnp.float32,
            )
            for i in range(4):
                coded, scale = encode(part[i * P_DEV:(i + 1) * P_DEV])
                d_out[first + i, :, columns(j)] = coded
                d_out_sc[first + i, :, columns(j)] = scale
            return carry

        lax.fori_loop(0, W // CB, block, 0)

        @pl.when(shifted)
        def _():
            for i in range(4):
                for copy in d_copies(first + i):
                    copy.start()

    def mirror_half(first):
        for slot in reversed(range(first, first + 4)):
            @pl.when(shifted)
            def _(slot=slot):
                far_copy(slot).wait_recv()
                expand(far, slot, dense_far)

        def block(j, carry):
            @pl.when(shifted)
            def _():
                mirror[first * P_DEV:first * P_DEV + HALF, columns(j)] = lax.dot_general(
                    dense_far[first * P_DEV:first * P_DEV + HALF, :], v_mir[columns(j), :],
                    (((1,), (1,)), ((), ())), preferred_element_type=jnp.float32,
                )

            @pl.when(z == 0)
            def _():
                mirror[first * P_DEV:first * P_DEV + HALF, columns(j)] = lax.dot_general(
                    dense_own[first * P_DEV:first * P_DEV + HALF, :], v_mir[columns(j), :],
                    (((1,), (1,)), ((), ())), preferred_element_type=jnp.float32,
                )
            return carry

        lax.fori_loop(0, W // CB, block, 0)

    direct_half(0)
    direct_half(4)
    mirror_half(4)
    mirror_half(0)

    def settle(slot, lanes, last):
        @pl.when(shifted)
        def _():
            for copy in d_copies(slot):
                copy.wait_recv()

        def block(j, carry):
            cols = columns(j)
            total = mirror[slot * P_DEV:(slot + 1) * P_DEV, cols]
            for lane in lanes:
                total = total + decode(r_in[lane, slot, :, cols], r_in_sc[lane, slot, :, cols])

            def finish(total):
                if last:
                    out_ref[:, cols] = total
                else:
                    coded, scale = encode(total)
                    r_out[slot, :, cols] = coded
                    r_out_sc[slot, :, cols] = scale

            @pl.when(shifted)
            def _():
                finish(total + decode(d_in[slot, :, cols], d_in_sc[slot, :, cols]))

            @pl.when(z == 0)
            def _():
                finish(total + decode(d_out[slot, :, cols], d_out_sc[slot, :, cols]))

            return carry

        lax.fori_loop(0, W // CB, block, 0)

    sum_sends = []
    for far_off in range(4, 0, -1):
        for step in (-1, 1):
            rel = far_off * step
            if rel == 4:
                continue
            slot = SLOT[rel]
            lanes = []
            if far_off < (4 if step == -1 else 3):
                for copy in r_copies(rel + step, step):
                    copy.wait_recv()
                lanes = [0 if step == 1 else 1]
            settle(slot, lanes, False)
            for copy in r_copies(rel, step):
                copy.start()
                sum_sends.append(copy)
    for step in (-1, 1):
        for copy in r_copies(step, step):
            copy.wait_recv()
    settle(me, [0, 1], True)

    for copy in gather_sends + sum_sends:
        copy.wait_send()

    @pl.when(shifted)
    def _():
        for slot in range(NB):
            far_copy(slot).wait_send()
            for copy in d_copies(slot):
                copy.wait_send()


def shards(l_tiles, nz_lists, v_slab):
    dma = pltpu.SemaphoreType.DMA
    return pl.pallas_call(
        kernel,
        out_shape=jax.ShapeDtypeStruct((P_DEV, W), jnp.float32),
        in_specs=[
            pl.BlockSpec(memory_space=pltpu.SMEM),
            pl.BlockSpec(memory_space=pltpu.VMEM),
            pl.BlockSpec(memory_space=pl.ANY),
        ],
        out_specs=pl.BlockSpec(memory_space=pltpu.VMEM),
        scratch_shapes=[
            pltpu.VMEM((NB, MSG, B), jnp.bfloat16),
            pltpu.VMEM((NB, MSG, B), jnp.bfloat16),
            pltpu.VMEM((NB * P_DEV, W), jnp.bfloat16),
            pltpu.VMEM((NB * P_DEV, W), jnp.bfloat16),
            pltpu.VMEM((W, W), jnp.bfloat16),
            pltpu.VMEM((W, W), jnp.bfloat16),
            pltpu.VMEM((NB * P_DEV, W), jnp.float32),
            pltpu.VMEM((NB, P_DEV, W), jnp.int16),
            pltpu.VMEM((NB, 1, W), jnp.float32),
            pltpu.VMEM((NB, P_DEV, W), jnp.int16),
            pltpu.VMEM((NB, 1, W), jnp.float32),
            pltpu.VMEM((NB, P_DEV, W), jnp.int16),
            pltpu.VMEM((NB, 1, W), jnp.float32),
            pltpu.VMEM((2, NB, P_DEV, W), jnp.int16),
            pltpu.VMEM((2, NB, 1, W), jnp.float32),
            dma((2,)),
            dma((NB,)), dma((NB,)),
            dma((NB,)), dma((NB,)),
            dma((NB,)), dma((NB,)), dma((NB,)), dma((NB,)),
            dma((NB,)), dma((2, NB)), dma((NB,)), dma((2, NB)),
        ],
        compiler_params=pltpu.CompilerParams(
            collective_id=0, has_side_effects=True, vmem_limit_bytes=48 << 20
        ),
    )(nz_lists, l_tiles, v_slab)


def solution(mesh):
    placed = (P("pair", "tile"), P("pair", "tile", None), P("tile", "pair", None, None))
    return jax.shard_map(
        shards, mesh=mesh, in_specs=placed, out_specs=P("pair", "tile"), check_vma=False
    )
```

```python
import functools

import jax
import jax.numpy as jnp
from jax import lax
from jax.experimental import pallas as pl
from jax.experimental.pallas import tpu as pltpu
from jax.sharding import PartitionSpec as P

MESH = pl.DeviceIdType.MESH
B = 128
KB = 10
NZ = 8
P_DEV = 96
W = B * KB
NB = 8
NG = 32
MSG = NZ * P_DEV + 16
CB = 256
HALF = 4 * P_DEV
REL = (4, 3, -3, 2, -2, 1, -1, 0)
SLOT = {rel: slot for slot, rel in enumerate(REL)}
SLOT[-4] = SLOT[4]
QMAX = 32767.0
SHARED = (4, 5)
LOW_TAKES = (0, -1, -2, -3)
LOW_GETS = (1, 2, 3, 4)
HIGH_TAKES = (0, 1, 2, 3)
HIGH_GETS = (-1, -2, -3, 4)


def near(rel):
    return (rel + 3) % NB - 3


def either(flags):
    return functools.reduce(jnp.logical_or, flags)


def encode(values):
    top = jnp.maximum(jnp.max(jnp.abs(values), axis=0, keepdims=True), 1e-30)
    coded = jnp.round(values * (QMAX / top)).astype(jnp.int32).astype(jnp.int16)
    return coded, top * (1.0 / QMAX)


def decode(coded, scale):
    return coded.astype(jnp.int32).astype(jnp.float32) * scale


def columns(j):
    return pl.ds(pl.multiple_of(j * CB, CB), CB)


def kernel(
    nz_ref, l_ref, v_ref, out_ref,
    lists, own, far, dense_own, dense_far, v_dir, v_mir, mirror,
    d_out, d_out_sc, d_in, d_in_sc, r_out, r_out_sc, r_in, r_in_sc, p_in, p_in_sc,
    l_sem, v_sem, ag_s, ag_r, far_s, far_r, d_s, d_r, dsc_s, dsc_r, r_s, r_r, rsc_s, rsc_r,
    fwd_s, p_s, p_r, psc_s, psc_r,
):
    t = lax.axis_index("tile")
    z = lax.axis_index("pair")
    up = (t, lax.rem(z + 1, NB))
    down = (t, lax.rem(z + NB - 1, NB))
    ahead = (lax.rem(t + z, NG), z)
    behind = (lax.rem(t + NG - z, NG), z)
    shifted = z > 0

    core = lax.rem(t, 2)
    core_behind = lax.rem(t + z, 2)
    plane_low = either([z == k - 1 for k in SHARED])
    plane_high = either([z == k for k in SHARED])
    low = (core == 1) & plane_low
    high = (core == 0) & plane_high
    mate = (t + 1 - 2 * core, z + 2 * core - 1)
    behind_low = (core_behind == 1) & plane_low
    behind_high = (core_behind == 0) & plane_high

    def behind_takes(rel):
        flag = shifted
        if rel in LOW_GETS:
            flag = flag & jnp.logical_not(behind_low)
        if rel in HIGH_GETS:
            flag = flag & jnp.logical_not(behind_high)
        return flag

    def handed(rel):
        flags = []
        if rel in LOW_GETS:
            flags.append(low)
        if rel in HIGH_GETS:
            flags.append(high)
        return flags

    me = SLOT[0]
    list_load = pltpu.make_async_copy(nz_ref, lists, l_sem.at[NZ])
    tile_loads = [
        pltpu.make_async_copy(
            l_ref.at[:, e * B:(e + 1) * B], own.at[me, e * P_DEV:(e + 1) * P_DEV, :], l_sem.at[e]
        )
        for e in range(NZ)
    ]
    list_load.start()
    for load in tile_loads:
        load.start()
    loads = [
        pltpu.make_async_copy(v_ref.at[0, 0], v_dir, v_sem.at[0]),
        pltpu.make_async_copy(v_ref.at[0, 0], v_mir, v_sem.at[1]),
    ]
    for load in loads:
        load.start()

    barrier = pltpu.get_barrier_semaphore()
    for device in (up, down):
        pl.semaphore_signal(barrier, inc=1, device_id=device, device_id_type=MESH)

    @pl.when(shifted)
    def _():
        for device in (ahead, behind):
            pl.semaphore_signal(barrier, inc=1, device_id=device, device_id_type=MESH)

    @pl.when(low | high)
    def _():
        pl.semaphore_signal(barrier, inc=1, device_id=mate, device_id_type=MESH)

    list_load.wait()
    entry = lax.broadcasted_iota(jnp.int32, (16, B), 0)
    listed = jnp.zeros((16, B), jnp.int32)
    for e in range(NZ):
        listed = jnp.where(entry == e, lists[0, 0, e], listed)
    own[me, NZ * P_DEV:, :] = listed.astype(jnp.float32).astype(jnp.bfloat16)

    pl.semaphore_wait(barrier, 2 + 2 * jnp.minimum(z, 1) + (low | high).astype(jnp.int32))
    for load in tile_loads:
        load.wait()

    def remote(src, dst, send, recv, device):
        return pltpu.make_async_remote_copy(
            src_ref=src, dst_ref=dst, send_sem=send, recv_sem=recv,
            device_id=device, device_id_type=MESH,
        )

    def gather_copy(rel, step):
        src, dst = SLOT[rel], SLOT[rel - step]
        return remote(own.at[src], own.at[dst], ag_s.at[dst], ag_r.at[dst], up if step == 1 else down)

    def far_copy(slot):
        return remote(own.at[slot], far.at[slot], far_s.at[slot], far_r.at[slot], behind)

    def hand_far(rel, step):
        src, dst = SLOT[rel], SLOT[near(rel - step)]
        return remote(far.at[src], far.at[dst], fwd_s.at[src], far_r.at[dst], mate)

    def hand_part(rel, step):
        src, dst = SLOT[rel], SLOT[near(rel - step)]
        return (
            remote(d_out.at[src], p_in.at[dst], p_s.at[src], p_r.at[dst], mate),
            remote(d_out_sc.at[src], p_in_sc.at[dst], psc_s.at[src], psc_r.at[dst], mate),
        )

    def d_copies(slot):
        return (
            remote(d_out.at[slot], d_in.at[slot], d_s.at[slot], d_r.at[slot], ahead),
            remote(d_out_sc.at[slot], d_in_sc.at[slot], dsc_s.at[slot], dsc_r.at[slot], ahead),
        )

    def r_copies(rel, step):
        src, dst = SLOT[rel], SLOT[rel - step]
        lane = 0 if step == 1 else 1
        device = up if step == 1 else down
        return (
            remote(r_out.at[src], r_in.at[lane, dst], r_s.at[src], r_r.at[lane, dst], device),
            remote(r_out_sc.at[src], r_in_sc.at[lane, dst], rsc_s.at[src], rsc_r.at[lane, dst], device),
        )

    def expand(msg, slot, dense):
        lists = msg[slot, NZ * P_DEV:, :].astype(jnp.float32)
        for k in range(KB):
            total = None
            for e in range(max(0, k - KB + NZ), min(NZ - 1, k) + 1):
                hit = jnp.where(lists[e:e + 1, :] == float(k), 1.0, 0.0).astype(jnp.bfloat16)
                term = msg[slot, e * P_DEV:(e + 1) * P_DEV, :] * hit
                total = term if total is None else total + term
            dense[slot * P_DEV:(slot + 1) * P_DEV, k * B:(k + 1) * B] = total

    gather_sends = []

    def gather_start(rel, step):
        copy = gather_copy(rel, step)
        copy.start()
        gather_sends.append(copy)

    def far_start(slot):
        @pl.when(behind_takes(REL[slot]))
        def _():
            far_copy(slot).start()

    def far_pass(rel):
        for role, takes, step in ((low, LOW_TAKES, 1), (high, HIGH_TAKES, -1)):
            if rel in takes:
                @pl.when(role)
                def _(step=step):
                    far_copy(SLOT[rel]).wait_recv()
                    hand_far(rel, step).start()

    gather_start(0, 1)
    gather_start(0, -1)
    far_start(me)
    for load in loads:
        load.wait()

    @pl.when(z == 0)
    def _():
        def mask(i, carry):
            rows = pl.ds(pl.multiple_of(i * B, B), B)
            row_ids = lax.broadcasted_iota(jnp.int32, (B, W), 0) + i * B
            col_ids = lax.broadcasted_iota(jnp.int32, (B, W), 1)
            block = v_dir[rows, :].astype(jnp.float32)
            v_dir[rows, :] = jnp.where(row_ids <= col_ids, block, 0.0).astype(jnp.bfloat16)
            v_mir[rows, :] = jnp.where(row_ids < col_ids, block, 0.0).astype(jnp.bfloat16)
            return carry

        lax.fori_loop(0, KB, mask, 0)

    expand(own, me, dense_own)

    for r in range(1, 5):
        gather_copy(-r + 1, 1).wait_recv()
        if r < 4:
            gather_start(-r, 1)
        far_start(SLOT[-r])
        if r < 4:
            gather_copy(r - 1, -1).wait_recv()
            if r < 3:
                gather_start(r, -1)
            far_start(SLOT[r])
        expand(own, SLOT[-r], dense_own)
        if r < 4:
            expand(own, SLOT[r], dense_own)
        far_pass(1 - r)
        if r > 1:
            far_pass(r - 1)

    def d_send(slot):
        rel = REL[slot]
        paired = low | high

        @pl.when(shifted & jnp.logical_not(paired))
        def _():
            for copy in d_copies(slot):
                copy.start()

        for role, gets, step in ((low, LOW_GETS, 1), (high, HIGH_GETS, -1)):
            if rel in gets:
                @pl.when(role)
                def _(step=step):
                    for copy in hand_part(rel, step):
                        copy.start()

    def d_merge(slot):
        rel = REL[slot]
        roles = []
        if rel in LOW_TAKES:
            roles.append(low)
        if rel in HIGH_TAKES:
            roles.append(high)

        @pl.when(either(roles))
        def _():
            for copy in hand_part_in(slot):
                copy.wait_recv()

            def block(j, carry):
                cols = columns(j)
                coded, scale = encode(
                    decode(d_out[slot, :, cols], d_out_sc[slot, :, cols])
                    + decode(p_in[slot, :, cols], p_in_sc[slot, :, cols])
                )
                d_out[slot, :, cols] = coded
                d_out_sc[slot, :, cols] = scale
                return carry

            lax.fori_loop(0, W // CB, block, 0)
            for copy in d_copies(slot):
                copy.start()

    def hand_part_in(slot):
        return (
            remote(d_out.at[slot], p_in.at[slot], p_s.at[slot], p_r.at[slot], mate),
            remote(d_out_sc.at[slot], p_in_sc.at[slot], psc_s.at[slot], psc_r.at[slot], mate),
        )

    def direct_half(first):
        def block(j, carry):
            part = jnp.dot(
                dense_own[first * P_DEV:first * P_DEV + HALF, :], v_dir[:, columns(j)],
                preferred_element_type=jnp.float32,
            )
            for i in range(4):
                coded, scale = encode(part[i * P_DEV:(i + 1) * P_DEV])
                d_out[first + i, :, columns(j)] = coded
                d_out_sc[first + i, :, columns(j)] = scale
            return carry

        lax.fori_loop(0, W // CB, block, 0)

        for slot in range(first, first + 4):
            d_send(slot)

    def mirror_half(first):
        for slot in reversed(range(first, first + 4)):
            rel = REL[slot]
            fresh = shifted
            if rel in LOW_TAKES:
                fresh = fresh & jnp.logical_not(low)
            if rel in HIGH_TAKES:
                fresh = fresh & jnp.logical_not(high)

            @pl.when(fresh)
            def _(slot=slot):
                far_copy(slot).wait_recv()

            @pl.when(shifted)
            def _(slot=slot):
                expand(far, slot, dense_far)

        def block(j, carry):
            @pl.when(shifted)
            def _():
                mirror[first * P_DEV:first * P_DEV + HALF, columns(j)] = lax.dot_general(
                    dense_far[first * P_DEV:first * P_DEV + HALF, :], v_mir[columns(j), :],
                    (((1,), (1,)), ((), ())), preferred_element_type=jnp.float32,
                )

            @pl.when(z == 0)
            def _():
                mirror[first * P_DEV:first * P_DEV + HALF, columns(j)] = lax.dot_general(
                    dense_own[first * P_DEV:first * P_DEV + HALF, :], v_mir[columns(j), :],
                    (((1,), (1,)), ((), ())), preferred_element_type=jnp.float32,
                )
            return carry

        lax.fori_loop(0, W // CB, block, 0)

    direct_half(0)
    direct_half(4)
    mirror_half(4)
    for slot in range(1, NB):
        d_merge(slot)
    mirror_half(0)

    def settle(slot, lanes, last):
        def add_direct(part, part_sc):
            def block(j, carry):
                cols = columns(j)
                rows = pl.ds(slot * P_DEV, P_DEV)
                mirror[rows, cols] = mirror[rows, cols] + decode(part[slot, :, cols], part_sc[slot, :, cols])
                return carry

            lax.fori_loop(0, W // CB, block, 0)

        @pl.when(behind_takes(REL[slot]))
        def _():
            for copy in d_copies(slot):
                copy.wait_recv()
            add_direct(d_in, d_in_sc)

        @pl.when(z == 0)
        def _():
            add_direct(d_out, d_out_sc)

        def block(j, carry):
            cols = columns(j)
            total = mirror[slot * P_DEV:(slot + 1) * P_DEV, cols]
            for lane in lanes:
                total = total + decode(r_in[lane, slot, :, cols], r_in_sc[lane, slot, :, cols])

            if last:
                out_ref[:, cols] = total
            else:
                coded, scale = encode(total)
                r_out[slot, :, cols] = coded
                r_out_sc[slot, :, cols] = scale
            return carry

        lax.fori_loop(0, W // CB, block, 0)

    sum_sends = []
    for far_off in range(4, 0, -1):
        for step in (-1, 1):
            rel = far_off * step
            if rel == 4:
                continue
            slot = SLOT[rel]
            lanes = []
            if far_off < (4 if step == -1 else 3):
                for copy in r_copies(rel + step, step):
                    copy.wait_recv()
                lanes = [0 if step == 1 else 1]
            settle(slot, lanes, False)
            for copy in r_copies(rel, step):
                copy.start()
                sum_sends.append(copy)
    for step in (-1, 1):
        for copy in r_copies(step, step):
            copy.wait_recv()
    settle(me, [0, 1], True)

    for copy in gather_sends + sum_sends:
        copy.wait_send()

    for slot, rel in enumerate(REL):
        @pl.when(behind_takes(rel))
        def _(slot=slot):
            far_copy(slot).wait_send()

        direct_sent = shifted
        for flag in handed(rel):
            direct_sent = direct_sent & jnp.logical_not(flag)

        @pl.when(direct_sent)
        def _(slot=slot):
            for copy in d_copies(slot):
                copy.wait_send()

        for role, gets, takes, step in ((low, LOW_GETS, LOW_TAKES, 1), (high, HIGH_GETS, HIGH_TAKES, -1)):
            @pl.when(role)
            def _(rel=rel, gets=gets, step=step):
                if rel in gets:
                    for copy in hand_part(rel, step):
                        copy.wait_send()
                else:
                    hand_far(rel, step).wait_send()


def shards(l_tiles, nz_lists, v_slab):
    dma = pltpu.SemaphoreType.DMA
    return pl.pallas_call(
        kernel,
        out_shape=jax.ShapeDtypeStruct((P_DEV, W), jnp.float32),
        in_specs=[
            pl.BlockSpec(memory_space=pltpu.HBM),
            pl.BlockSpec(memory_space=pltpu.HBM),
            pl.BlockSpec(memory_space=pltpu.HBM),
        ],
        out_specs=pl.BlockSpec(memory_space=pltpu.VMEM),
        scratch_shapes=[
            pltpu.SMEM((1, 1, NZ), jnp.int32),
            pltpu.VMEM((NB, MSG, B), jnp.bfloat16),
            pltpu.VMEM((NB, MSG, B), jnp.bfloat16),
            pltpu.VMEM((NB * P_DEV, W), jnp.bfloat16),
            pltpu.VMEM((NB * P_DEV, W), jnp.bfloat16),
            pltpu.VMEM((W, W), jnp.bfloat16),
            pltpu.VMEM((W, W), jnp.bfloat16),
            pltpu.VMEM((NB * P_DEV, W), jnp.float32),
            pltpu.VMEM((NB, P_DEV, W), jnp.int16),
            pltpu.VMEM((NB, 1, W), jnp.float32),
            pltpu.VMEM((NB, P_DEV, W), jnp.int16),
            pltpu.VMEM((NB, 1, W), jnp.float32),
            pltpu.VMEM((NB, P_DEV, W), jnp.int16),
            pltpu.VMEM((NB, 1, W), jnp.float32),
            pltpu.VMEM((2, NB, P_DEV, W), jnp.int16),
            pltpu.VMEM((2, NB, 1, W), jnp.float32),
            pltpu.VMEM((NB, P_DEV, W), jnp.int16),
            pltpu.VMEM((NB, 1, W), jnp.float32),
            dma((NZ + 1,)),
            dma((2,)),
            dma((NB,)), dma((NB,)),
            dma((NB,)), dma((NB,)),
            dma((NB,)), dma((NB,)), dma((NB,)), dma((NB,)),
            dma((NB,)), dma((2, NB)), dma((NB,)), dma((2, NB)),
            dma((NB,)), dma((NB,)), dma((NB,)), dma((NB,)), dma((NB,)),
        ],
        compiler_params=pltpu.CompilerParams(
            collective_id=0, has_side_effects=True, vmem_limit_bytes=63 << 20
        ),
    )(nz_lists, l_tiles, v_slab)


def solution(mesh):
    placed = (P("pair", "tile"), P("pair", "tile", None), P("tile", "pair", None, None))
    return jax.shard_map(
        shards, mesh=mesh, in_specs=placed, out_specs=P("pair", "tile"), check_vma=False
    )
```

```python
import functools

import jax
import jax.numpy as jnp
from jax import lax
from jax.experimental import pallas as pl
from jax.experimental.pallas import tpu as pltpu
from jax.sharding import PartitionSpec as P

MESH = pl.DeviceIdType.MESH
B = 128
KB = 10
NZ = 8
P_DEV = 96
W = B * KB
NB = 8
NG = 32
MSG = NZ * P_DEV + 16
CB = 256
ROW_PIECES = ((0, 208), (208, 192), (400, 192), (592, 192))
ROWS_UP = 2
COL_PIECES = 2
PW = W // COL_PIECES
REL = (4, -3, 3, 2, -2, 1, -1, 0)
SLOT = {rel: slot for slot, rel in enumerate(REL)}
SLOT[-4] = SLOT[4]
QMAX = 32767.0
SHARED = (2, 3, 4, 5, 6, 7)
LOW_TAKES = (0, -1, -2, -3)
LOW_GETS = (1, 2, 3, 4)
HIGH_TAKES = (0, 1, 2, 3)
HIGH_GETS = (-1, -2, -3, 4)
MERGED = (2, 3, 4, 5, 6, 7)
LOW_MERGES = (0, -1, -2, -3)
LOW_LENDS = (1, 2, 3, 4)


def near(rel):
    return (rel + 3) % NB - 3


HIGH_MERGES = tuple(near(rel - 1) for rel in LOW_LENDS)
HIGH_LENDS = tuple(near(rel - 1) for rel in LOW_MERGES)


def either(flags):
    return functools.reduce(jnp.logical_or, flags)


def encode(values):
    top = jnp.maximum(jnp.max(jnp.abs(values), axis=0, keepdims=True), 1e-30)
    coded = jnp.round(values * (QMAX / top)).astype(jnp.int32).astype(jnp.int16)
    return coded, top * (1.0 / QMAX)


def decode(coded, scale):
    return coded.astype(jnp.int32).astype(jnp.float32) * scale


def columns(j):
    return pl.ds(pl.multiple_of(j * CB, CB), CB)


def kernel(
    nz_ref, l_ref, v_ref, out_ref,
    lists, own, far, dense_own, dense_far, v_dir, v_mir, mirror,
    d_out, d_out_sc, d_in, d_in_sc, r_out, r_out_sc, r_in, r_in_sc, p_in, p_in_sc,
    l_sem, v_sem, ag_s, ag_r, far_s, far_r, d_s, d_r, dsc_s, dsc_r, r_s, r_r, rsc_s, rsc_r,
    fwd_s, p_s, p_r, psc_s, psc_r,
):
    t = lax.axis_index("tile")
    z = lax.axis_index("pair")
    up = (t, lax.rem(z + 1, NB))
    down = (t, lax.rem(z + NB - 1, NB))
    ahead = (lax.rem(t + z, NG), z)
    behind = (lax.rem(t + NG - z, NG), z)
    shifted = z > 0

    core = lax.rem(t, 2)
    core_behind = lax.rem(t + z, 2)
    plane_low = either([z == k - 1 for k in SHARED])
    plane_high = either([z == k for k in SHARED])
    low = (core == 1) & plane_low
    high = (core == 0) & plane_high
    mate = (t + 1 - 2 * core, z + 2 * core - 1)
    low_d = (core == 1) & either([z == k - 1 for k in MERGED])
    high_d = (core == 0) & either([z == k for k in MERGED])
    behind_low_d = (core_behind == 1) & either([z == k - 1 for k in MERGED])
    behind_high_d = (core_behind == 0) & either([z == k for k in MERGED])
    behind_low = (core_behind == 1) & plane_low
    behind_high = (core_behind == 0) & plane_high

    def behind_takes(rel):
        flag = shifted
        if rel in LOW_GETS:
            flag = flag & jnp.logical_not(behind_low)
        if rel in HIGH_GETS:
            flag = flag & jnp.logical_not(behind_high)
        return flag

    def behind_sends(rel):
        flag = shifted
        if rel in LOW_LENDS:
            flag = flag & jnp.logical_not(behind_low_d)
        if rel in HIGH_LENDS:
            flag = flag & jnp.logical_not(behind_high_d)
        return flag

    def lent(rel):
        flag = z < 0
        if rel in LOW_LENDS:
            flag = flag | low_d
        if rel in HIGH_LENDS:
            flag = flag | high_d
        return flag

    def merges(rel):
        flag = z < 0
        if rel in LOW_MERGES:
            flag = flag | low_d
        if rel in HIGH_MERGES:
            flag = flag | high_d
        return flag

    me = SLOT[0]
    list_load = pltpu.make_async_copy(nz_ref, lists, l_sem.at[NZ])
    tile_loads = [
        pltpu.make_async_copy(
            l_ref.at[:, e * B:(e + 1) * B], own.at[me, e * P_DEV:(e + 1) * P_DEV, :], l_sem.at[e]
        )
        for e in range(NZ)
    ]
    list_load.start()
    for load in tile_loads:
        load.start()
    v_load = pltpu.make_async_copy(v_ref.at[0, 0], v_dir, v_sem.at[0])
    v_load.start()

    barrier = pltpu.get_barrier_semaphore()
    for device in (up, down):
        pl.semaphore_signal(barrier, inc=1, device_id=device, device_id_type=MESH)

    @pl.when(shifted)
    def _():
        for device in (ahead, behind):
            pl.semaphore_signal(barrier, inc=1, device_id=device, device_id_type=MESH)

    @pl.when(low | high)
    def _():
        pl.semaphore_signal(barrier, inc=1, device_id=mate, device_id_type=MESH)

    list_load.wait()
    entry = lax.broadcasted_iota(jnp.int32, (16, B), 0)
    listed = jnp.zeros((16, B), jnp.int32)
    for e in range(NZ):
        listed = jnp.where(entry == e, lists[0, 0, e], listed)
    own[me, NZ * P_DEV:, :] = listed.astype(jnp.float32).astype(jnp.bfloat16)

    pl.semaphore_wait(barrier, 2 + 2 * jnp.minimum(z, 1) + (low | high).astype(jnp.int32))
    for load in tile_loads:
        load.wait()

    def remote(src, dst, send, recv, device):
        return pltpu.make_async_remote_copy(
            src_ref=src, dst_ref=dst, send_sem=send, recv_sem=recv,
            device_id=device, device_id_type=MESH,
        )

    def gather_copy(rel, step, piece):
        src, dst = SLOT[rel], SLOT[rel - step]
        rows = pl.ds(*ROW_PIECES[piece])
        return remote(
            own.at[src, rows], own.at[dst, rows], ag_s.at[dst, piece], ag_r.at[dst, piece],
            up if step == 1 else down,
        )

    def far_copy(slot):
        return remote(own.at[slot], far.at[slot], far_s.at[slot], far_r.at[slot], behind)

    def hand_far(rel, step):
        src, dst = SLOT[rel], SLOT[near(rel - step)]
        return remote(far.at[src], far.at[dst], fwd_s.at[src], far_r.at[dst], mate)

    def hand_part(rel, step):
        src, dst = SLOT[rel], SLOT[near(rel - step)]
        return (
            remote(d_out.at[src], p_in.at[dst], p_s.at[src], p_r.at[dst], mate),
            remote(d_out_sc.at[src], p_in_sc.at[dst], psc_s.at[src], psc_r.at[dst], mate),
        )

    def d_copies(slot):
        return (
            remote(d_out.at[slot], d_in.at[slot], d_s.at[slot], d_r.at[slot], ahead),
            remote(d_out_sc.at[slot], d_in_sc.at[slot], dsc_s.at[slot], dsc_r.at[slot], ahead),
        )

    def r_copies(rel, step, piece):
        src, dst = SLOT[rel], SLOT[rel - step]
        lane = 0 if step == 1 else 1
        device = up if step == 1 else down
        cols = pl.ds(piece * PW, PW)
        return (
            remote(
                r_out.at[src, :, cols], r_in.at[lane, dst, :, cols],
                r_s.at[src, piece], r_r.at[lane, dst, piece], device,
            ),
            remote(
                r_out_sc.at[src, :, cols], r_in_sc.at[lane, dst, :, cols],
                rsc_s.at[src, piece], rsc_r.at[lane, dst, piece], device,
            ),
        )

    def expand(msg, slot, dense):
        lists = msg[slot, NZ * P_DEV:, :].astype(jnp.float32)
        for k in range(KB):
            total = None
            for e in range(max(0, k - KB + NZ), min(NZ - 1, k) + 1):
                hit = jnp.where(lists[e:e + 1, :] == float(k), 1.0, 0.0).astype(jnp.bfloat16)
                term = msg[slot, e * P_DEV:(e + 1) * P_DEV, :] * hit
                total = term if total is None else total + term
            dense[slot * P_DEV:(slot + 1) * P_DEV, k * B:(k + 1) * B] = total

    gather_sends = []

    def gather_start(rel, step, piece):
        copy = gather_copy(rel, step, piece)
        copy.start()
        gather_sends.append(copy)

    def far_start(slot):
        @pl.when(behind_takes(REL[slot]))
        def _():
            far_copy(slot).start()

    def far_pass(rel):
        for role, takes, step in ((low, LOW_TAKES, 1), (high, HIGH_TAKES, -1)):
            if rel in takes:
                @pl.when(role)
                def _(step=step):
                    far_copy(SLOT[rel]).wait_recv()
                    hand_far(rel, step).start()

    for piece in range(len(ROW_PIECES)):
        gather_start(0, 1, piece)
        gather_start(0, -1, piece)
    far_start(me)
    v_load.wait()

    def turn(i, carry):
        rows = pl.ds(pl.multiple_of(i * B, B), B)

        @pl.when(shifted)
        def _():
            v_mir[:, rows] = v_dir[rows, :].T

        @pl.when(z == 0)
        def _():
            row_ids = lax.broadcasted_iota(jnp.int32, (B, W), 0) + i * B
            col_ids = lax.broadcasted_iota(jnp.int32, (B, W), 1)
            block = v_dir[rows, :].astype(jnp.float32)
            v_dir[rows, :] = jnp.where(row_ids <= col_ids, block, 0.0).astype(jnp.bfloat16)
            v_mir[:, rows] = jnp.where(row_ids < col_ids, block, 0.0).astype(jnp.bfloat16).T

        return carry

    lax.fori_loop(0, KB, turn, 0)
    expand(own, me, dense_own)

    def d_send(rel):
        slot = SLOT[rel]

        @pl.when(shifted & jnp.logical_not(lent(rel)) & jnp.logical_not(merges(rel)))
        def _():
            for copy in d_copies(slot):
                copy.start()

    def d_lend(rel):
        for role, lends, step in ((low_d, LOW_LENDS, 1), (high_d, HIGH_LENDS, -1)):
            if rel in lends:
                @pl.when(role)
                def _(step=step):
                    for copy in hand_part(rel, step):
                        copy.start()

    def d_merge(rel):
        slot = SLOT[rel]
        if rel not in LOW_MERGES + HIGH_MERGES:
            return

        @pl.when(merges(rel))
        def _():
            for copy in hand_part_in(slot):
                copy.wait_recv()

            def block(j, carry):
                cols = columns(j)
                coded, scale = encode(
                    decode(d_out[slot, :, cols], d_out_sc[slot, :, cols])
                    + decode(p_in[slot, :, cols], p_in_sc[slot, :, cols])
                )
                d_out[slot, :, cols] = coded
                d_out_sc[slot, :, cols] = scale
                return carry

            lax.fori_loop(0, W // CB, block, 0)
            for copy in d_copies(slot):
                copy.start()

    def hand_part_in(slot):
        return (
            remote(d_out.at[slot], p_in.at[slot], p_s.at[slot], p_r.at[slot], mate),
            remote(d_out_sc.at[slot], p_in_sc.at[slot], psc_s.at[slot], psc_r.at[slot], mate),
        )

    def direct(first, last):
        count = last - first + 1

        def block(j, carry):
            part = jnp.dot(
                dense_own[first * P_DEV:(last + 1) * P_DEV, :], v_dir[:, columns(j)],
                preferred_element_type=jnp.float32,
            )
            for i in range(count):
                coded, scale = encode(part[i * P_DEV:(i + 1) * P_DEV])
                d_out[first + i, :, columns(j)] = coded
                d_out_sc[first + i, :, columns(j)] = scale
            return carry

        lax.fori_loop(0, W // CB, block, 0)

    def far_wait(slot):
        rel = REL[slot]
        fresh = shifted
        if rel in LOW_TAKES:
            fresh = fresh & jnp.logical_not(low)
        if rel in HIGH_TAKES:
            fresh = fresh & jnp.logical_not(high)

        @pl.when(fresh)
        def _():
            far_copy(slot).wait_recv()

        @pl.when(shifted)
        def _():
            expand(far, slot, dense_far)

    def mirrored(first, last):
        for slot in range(last, first - 1, -1):
            far_wait(slot)
        rows = slice(first * P_DEV, (last + 1) * P_DEV)

        def block(j, carry):
            for flag, dense in ((shifted, dense_far), (z == 0, dense_own)):
                @pl.when(flag)
                def _(dense=dense):
                    mirror[rows, columns(j)] = jnp.dot(
                        dense[rows, :], v_mir[:, columns(j)], preferred_element_type=jnp.float32
                    )
            return carry

        lax.fori_loop(0, W // CB, block, 0)

    def gathered(r):
        for piece in range(len(ROW_PIECES)):
            if r < 4 or piece < ROWS_UP:
                gather_copy(-r + 1, 1, piece).wait_recv()
            if r < 3 or (r == 3 and piece < ROWS_UP):
                gather_start(-r, 1, piece)
            if r < 4 or piece >= ROWS_UP:
                gather_copy(r - 1, -1, piece).wait_recv()
            if r < 3 or (r == 3 and piece >= ROWS_UP):
                gather_start(r, -1, piece)

    direct(7, 7)
    gathered(1)
    far_start(SLOT[-1])
    far_start(SLOT[1])
    expand(own, SLOT[-1], dense_own)
    expand(own, SLOT[1], dense_own)
    direct(5, 6)
    d_send(1)
    d_send(-1)
    far_pass(0)
    gathered(2)
    far_start(SLOT[-2])
    expand(own, SLOT[-2], dense_own)
    expand(own, SLOT[2], dense_own)
    direct(3, 4)
    d_send(2)
    far_pass(-1)
    far_pass(1)
    gathered(3)
    far_start(SLOT[-3])
    expand(own, SLOT[-3], dense_own)
    expand(own, SLOT[3], dense_own)
    far_pass(-2)
    gathered(4)
    far_start(SLOT[4])
    far_start(SLOT[3])
    far_start(SLOT[2])
    expand(own, SLOT[4], dense_own)
    direct(0, 2)
    d_send(4)
    d_lend(4)
    d_send(-3)
    d_lend(-3)
    d_send(3)
    d_lend(3)
    d_lend(2)
    d_lend(-2)
    d_lend(1)
    d_lend(-1)
    far_pass(-3)
    far_pass(3)
    far_pass(2)

    def add_direct(slot):
        def add(part, part_sc):
            def block(j, carry):
                cols = columns(j)
                rows = pl.ds(slot * P_DEV, P_DEV)
                mirror[rows, cols] = mirror[rows, cols] + decode(part[slot, :, cols], part_sc[slot, :, cols])
                return carry

            lax.fori_loop(0, W // CB, block, 0)

        @pl.when(behind_sends(REL[slot]))
        def _():
            for copy in d_copies(slot):
                copy.wait_recv()
            add(d_in, d_in_sc)

        @pl.when(z == 0)
        def _():
            add(d_out, d_out_sc)

    def settle(slot, piece, lanes, last):
        def block(j, carry):
            cols = pl.ds(pl.multiple_of(piece * PW + j * B, B), B)
            total = mirror[slot * P_DEV:(slot + 1) * P_DEV, cols]
            for lane in lanes:
                total = total + decode(r_in[lane, slot, :, cols], r_in_sc[lane, slot, :, cols])
            if last:
                out_ref[:, cols] = total
            else:
                coded, scale = encode(total)
                r_out[slot, :, cols] = coded
                r_out_sc[slot, :, cols] = scale
            return carry

        lax.fori_loop(0, PW // B, block, 0)

    sum_sends = []

    def relay(far_off):
        for slot in sorted({SLOT[far_off], SLOT[-far_off]}):
            add_direct(slot)
        for step, piece in ((1, 0), (-1, 1), (-1, 0), (1, 1)):
            begins = (step, piece) in ((1, 0), (-1, 1))
            if far_off == 4 and begins:
                continue
            rel = far_off * step
            lanes = []
            if far_off < 3 or (far_off == 3 and not begins):
                for copy in r_copies(rel + step, step, piece):
                    copy.wait_recv()
                lanes = [0 if step == 1 else 1]
            settle(SLOT[rel], piece, lanes, False)
            for copy in r_copies(rel, step, piece):
                copy.start()
                sum_sends.append(copy)

    mirrored(4, 7)
    d_merge(-3)
    d_merge(3)
    mirrored(0, 0)
    relay(4)
    d_send(-2)
    d_merge(-2)
    d_merge(2)
    mirrored(1, 2)
    relay(3)
    d_send(0)
    d_merge(-1)
    d_merge(1)
    d_merge(0)
    mirrored(3, 3)
    relay(2)
    relay(1)
    add_direct(me)
    for piece in range(COL_PIECES):
        for step in (-1, 1):
            for copy in r_copies(step, step, piece):
                copy.wait_recv()
        settle(me, piece, [0, 1], True)

    for copy in gather_sends + sum_sends:
        copy.wait_send()

    for slot, rel in enumerate(REL):
        @pl.when(behind_takes(rel))
        def _(slot=slot):
            far_copy(slot).wait_send()

        @pl.when(shifted & jnp.logical_not(lent(rel)))
        def _(slot=slot):
            for copy in d_copies(slot):
                copy.wait_send()

        for role, takes, step in ((low, LOW_TAKES, 1), (high, HIGH_TAKES, -1)):
            if rel in takes:
                @pl.when(role)
                def _(rel=rel, step=step):
                    hand_far(rel, step).wait_send()

        for role, lends, step in ((low_d, LOW_LENDS, 1), (high_d, HIGH_LENDS, -1)):
            if rel in lends:
                @pl.when(role)
                def _(rel=rel, step=step):
                    for copy in hand_part(rel, step):
                        copy.wait_send()


def shards(l_tiles, nz_lists, v_slab):
    dma = pltpu.SemaphoreType.DMA
    return pl.pallas_call(
        kernel,
        out_shape=jax.ShapeDtypeStruct((P_DEV, W), jnp.float32),
        in_specs=[
            pl.BlockSpec(memory_space=pltpu.HBM),
            pl.BlockSpec(memory_space=pltpu.HBM),
            pl.BlockSpec(memory_space=pltpu.HBM),
        ],
        out_specs=pl.BlockSpec(memory_space=pltpu.VMEM),
        scratch_shapes=[
            pltpu.SMEM((1, 1, NZ), jnp.int32),
            pltpu.VMEM((NB, MSG, B), jnp.bfloat16),
            pltpu.VMEM((NB, MSG, B), jnp.bfloat16),
            pltpu.VMEM((NB * P_DEV, W), jnp.bfloat16),
            pltpu.VMEM((NB * P_DEV, W), jnp.bfloat16),
            pltpu.VMEM((W, W), jnp.bfloat16),
            pltpu.VMEM((W, W), jnp.bfloat16),
            pltpu.VMEM((NB * P_DEV, W), jnp.float32),
            pltpu.VMEM((NB, P_DEV, W), jnp.int16),
            pltpu.VMEM((NB, 1, W), jnp.float32),
            pltpu.VMEM((NB, P_DEV, W), jnp.int16),
            pltpu.VMEM((NB, 1, W), jnp.float32),
            pltpu.VMEM((NB, P_DEV, W), jnp.int16),
            pltpu.VMEM((NB, 1, W), jnp.float32),
            pltpu.VMEM((2, NB, P_DEV, W), jnp.int16),
            pltpu.VMEM((2, NB, 1, W), jnp.float32),
            pltpu.VMEM((NB, P_DEV, W), jnp.int16),
            pltpu.VMEM((NB, 1, W), jnp.float32),
            dma((NZ + 1,)),
            dma((1,)),
            dma((NB, len(ROW_PIECES))), dma((NB, len(ROW_PIECES))),
            dma((NB,)), dma((NB,)),
            dma((NB,)), dma((NB,)), dma((NB,)), dma((NB,)),
            dma((NB, 2)), dma((2, NB, 2)), dma((NB, 2)), dma((2, NB, 2)),
            dma((NB,)), dma((NB,)), dma((NB,)), dma((NB,)), dma((NB,)),
        ],
        compiler_params=pltpu.CompilerParams(
            collective_id=0, has_side_effects=True, vmem_limit_bytes=63 << 20
        ),
    )(nz_lists, l_tiles, v_slab)


def solution(mesh):
    placed = (P("pair", "tile"), P("pair", "tile", None), P("tile", "pair", None, None))
    return jax.shard_map(
        shards, mesh=mesh, in_specs=placed, out_specs=P("pair", "tile"), check_vma=False
    )
```

```python
import functools

import jax
import jax.numpy as jnp
from jax import lax
from jax.experimental import pallas as pl
from jax.experimental.pallas import tpu as pltpu
from jax.sharding import PartitionSpec as P

MESH = pl.DeviceIdType.MESH
B = 128
KB = 10
NZ = 8
P_DEV = 96
W = B * KB
NB = 8
NG = 32
MSG = NZ * P_DEV + 16
CB = 256
ROW_PIECES = ((0, 208), (208, 192), (400, 192), (592, 192))
ROWS_UP = 2
COL_PIECES = 2
PW = W // COL_PIECES
REL = (4, -3, 3, 2, -2, 1, -1, 0)
SLOT = {rel: slot for slot, rel in enumerate(REL)}
SLOT[-4] = SLOT[4]
QMAX = 32767.0
SHARED = (2, 3, 4, 5, 6, 7)
LOW_TAKES = (0, -1, -2, -3)
LOW_GETS = (1, 2, 3, 4)
HIGH_TAKES = (0, 1, 2, 3)
HIGH_GETS = (-1, -2, -3, 4)
MERGED = (2, 3, 4, 5, 6, 7)
LOW_MERGES = (0, -1, -2)
LOW_LENDS = (1, 2, 3)


def near(rel):
    return (rel + 3) % NB - 3


HIGH_MERGES = tuple(near(rel - 1) for rel in LOW_LENDS)
HIGH_LENDS = tuple(near(rel - 1) for rel in LOW_MERGES)


def either(flags):
    return functools.reduce(jnp.logical_or, flags)


def encode(values):
    top = jnp.maximum(jnp.max(jnp.abs(values), axis=0, keepdims=True), 1e-30)
    coded = jnp.round(values * (QMAX / top)).astype(jnp.int32).astype(jnp.int16)
    return coded, top * (1.0 / QMAX)


def decode(coded, scale):
    return coded.astype(jnp.int32).astype(jnp.float32) * scale


def columns(j):
    return pl.ds(pl.multiple_of(j * CB, CB), CB)


def kernel(
    nz_ref, l_ref, v_ref, out_ref,
    lists, own, far, dense_own, dense_far, v_dir, v_mir, mirror,
    d_out, d_out_sc, d_in, d_in_sc, r_out, r_out_sc, r_in, r_in_sc, p_in, p_in_sc,
    l_sem, v_sem, ag_s, ag_r, far_s, far_r, d_s, d_r, dsc_s, dsc_r, r_s, r_r, rsc_s, rsc_r,
    fwd_s, p_s, p_r, psc_s, psc_r,
):
    t = lax.axis_index("tile")
    z = lax.axis_index("pair")
    up = (t, lax.rem(z + 1, NB))
    down = (t, lax.rem(z + NB - 1, NB))
    ahead = (lax.rem(t + z, NG), z)
    behind = (lax.rem(t + NG - z, NG), z)
    shifted = z > 0

    core = lax.rem(t, 2)
    core_behind = lax.rem(t + z, 2)
    plane_low = either([z == k - 1 for k in SHARED])
    plane_high = either([z == k for k in SHARED])
    low = (core == 1) & plane_low
    high = (core == 0) & plane_high
    mate = (t + 1 - 2 * core, z + 2 * core - 1)
    low_d = (core == 1) & either([z == k - 1 for k in MERGED])
    high_d = (core == 0) & either([z == k for k in MERGED])
    behind_low_d = (core_behind == 1) & either([z == k - 1 for k in MERGED])
    behind_high_d = (core_behind == 0) & either([z == k for k in MERGED])
    behind_low = (core_behind == 1) & plane_low
    behind_high = (core_behind == 0) & plane_high

    def behind_takes(rel):
        flag = shifted
        if rel in LOW_GETS:
            flag = flag & jnp.logical_not(behind_low)
        if rel in HIGH_GETS:
            flag = flag & jnp.logical_not(behind_high)
        return flag

    def behind_sends(rel):
        flag = shifted
        if rel in LOW_LENDS:
            flag = flag & jnp.logical_not(behind_low_d)
        if rel in HIGH_LENDS:
            flag = flag & jnp.logical_not(behind_high_d)
        return flag

    def lent(rel):
        flag = z < 0
        if rel in LOW_LENDS:
            flag = flag | low_d
        if rel in HIGH_LENDS:
            flag = flag | high_d
        return flag

    def merges(rel):
        flag = z < 0
        if rel in LOW_MERGES:
            flag = flag | low_d
        if rel in HIGH_MERGES:
            flag = flag | high_d
        return flag

    me = SLOT[0]
    list_load = pltpu.make_async_copy(nz_ref, lists, l_sem.at[NZ])
    tile_loads = [
        pltpu.make_async_copy(
            l_ref.at[:, e * B:(e + 1) * B], own.at[me, e * P_DEV:(e + 1) * P_DEV, :], l_sem.at[e]
        )
        for e in range(NZ)
    ]
    list_load.start()
    for load in tile_loads:
        load.start()
    v_load = pltpu.make_async_copy(v_ref.at[0, 0], v_dir, v_sem.at[0])
    v_load.start()

    barrier = pltpu.get_barrier_semaphore()
    for device in (up, down):
        pl.semaphore_signal(barrier, inc=1, device_id=device, device_id_type=MESH)

    @pl.when(shifted)
    def _():
        for device in (ahead, behind):
            pl.semaphore_signal(barrier, inc=1, device_id=device, device_id_type=MESH)

    @pl.when(low | high)
    def _():
        pl.semaphore_signal(barrier, inc=1, device_id=mate, device_id_type=MESH)

    list_load.wait()
    entry = lax.broadcasted_iota(jnp.int32, (16, B), 0)
    listed = jnp.zeros((16, B), jnp.int32)
    for e in range(NZ):
        listed = jnp.where(entry == e, lists[0, 0, e], listed)
    own[me, NZ * P_DEV:, :] = listed.astype(jnp.float32).astype(jnp.bfloat16)

    pl.semaphore_wait(barrier, 2 + 2 * jnp.minimum(z, 1) + (low | high).astype(jnp.int32))
    for load in tile_loads:
        load.wait()

    def remote(src, dst, send, recv, device):
        return pltpu.make_async_remote_copy(
            src_ref=src, dst_ref=dst, send_sem=send, recv_sem=recv,
            device_id=device, device_id_type=MESH,
        )

    def gather_copy(rel, step, piece):
        src, dst = SLOT[rel], SLOT[rel - step]
        rows = pl.ds(*ROW_PIECES[piece])
        return remote(
            own.at[src, rows], own.at[dst, rows], ag_s.at[dst, piece], ag_r.at[dst, piece],
            up if step == 1 else down,
        )

    def far_copy(slot):
        return remote(own.at[slot], far.at[slot], far_s.at[slot], far_r.at[slot], behind)

    def hand_far(rel, step):
        src, dst = SLOT[rel], SLOT[near(rel - step)]
        return remote(far.at[src], far.at[dst], fwd_s.at[src], far_r.at[dst], mate)

    def hand_part(rel, step):
        src, dst = SLOT[rel], SLOT[near(rel - step)]
        return (
            remote(d_out.at[src], p_in.at[dst], p_s.at[src], p_r.at[dst], mate),
            remote(d_out_sc.at[src], p_in_sc.at[dst], psc_s.at[src], psc_r.at[dst], mate),
        )

    def d_copies(slot):
        return (
            remote(d_out.at[slot], d_in.at[slot], d_s.at[slot], d_r.at[slot], ahead),
            remote(d_out_sc.at[slot], d_in_sc.at[slot], dsc_s.at[slot], dsc_r.at[slot], ahead),
        )

    def r_copies(rel, step, piece):
        src, dst = SLOT[rel], SLOT[rel - step]
        lane = 0 if step == 1 else 1
        device = up if step == 1 else down
        cols = pl.ds(piece * PW, PW)
        return (
            remote(
                r_out.at[src, :, cols], r_in.at[lane, dst, :, cols],
                r_s.at[src, piece], r_r.at[lane, dst, piece], device,
            ),
            remote(
                r_out_sc.at[src, :, cols], r_in_sc.at[lane, dst, :, cols],
                rsc_s.at[src, piece], rsc_r.at[lane, dst, piece], device,
            ),
        )

    def expand(msg, slot, dense):
        lists = msg[slot, NZ * P_DEV:, :].astype(jnp.float32)
        for k in range(KB):
            total = None
            for e in range(max(0, k - KB + NZ), min(NZ - 1, k) + 1):
                hit = jnp.where(lists[e:e + 1, :] == float(k), 1.0, 0.0).astype(jnp.bfloat16)
                term = msg[slot, e * P_DEV:(e + 1) * P_DEV, :] * hit
                total = term if total is None else total + term
            dense[slot * P_DEV:(slot + 1) * P_DEV, k * B:(k + 1) * B] = total

    gather_sends = []

    def gather_start(rel, step, piece):
        copy = gather_copy(rel, step, piece)
        copy.start()
        gather_sends.append(copy)

    def far_start(slot):
        @pl.when(behind_takes(REL[slot]))
        def _():
            far_copy(slot).start()

    def far_pass(rel):
        for role, takes, step in ((low, LOW_TAKES, 1), (high, HIGH_TAKES, -1)):
            if rel in takes:
                @pl.when(role)
                def _(step=step):
                    far_copy(SLOT[rel]).wait_recv()
                    hand_far(rel, step).start()

    for piece in range(len(ROW_PIECES)):
        gather_start(0, 1, piece)
        gather_start(0, -1, piece)
    far_start(me)
    v_load.wait()

    def turn(i, carry):
        rows = pl.ds(pl.multiple_of(i * B, B), B)

        @pl.when(shifted)
        def _():
            v_mir[:, rows] = v_dir[rows, :].T

        @pl.when(z == 0)
        def _():
            row_ids = lax.broadcasted_iota(jnp.int32, (B, W), 0) + i * B
            col_ids = lax.broadcasted_iota(jnp.int32, (B, W), 1)
            block = v_dir[rows, :].astype(jnp.float32)
            v_dir[rows, :] = jnp.where(row_ids <= col_ids, block, 0.0).astype(jnp.bfloat16)
            v_mir[:, rows] = jnp.where(row_ids < col_ids, block, 0.0).astype(jnp.bfloat16).T

        return carry

    lax.fori_loop(0, KB, turn, 0)
    expand(own, me, dense_own)

    def d_send(rel):
        slot = SLOT[rel]

        @pl.when(shifted & jnp.logical_not(lent(rel)) & jnp.logical_not(merges(rel)))
        def _():
            for copy in d_copies(slot):
                copy.start()

    def d_lend(rel):
        for role, lends, step in ((low_d, LOW_LENDS, 1), (high_d, HIGH_LENDS, -1)):
            if rel in lends:
                @pl.when(role)
                def _(step=step):
                    for copy in hand_part(rel, step):
                        copy.start()

    def d_merge(rel):
        slot = SLOT[rel]
        if rel not in LOW_MERGES + HIGH_MERGES:
            return

        @pl.when(merges(rel))
        def _():
            for copy in hand_part_in(slot):
                copy.wait_recv()

            def block(j, carry):
                cols = columns(j)
                coded, scale = encode(
                    decode(d_out[slot, :, cols], d_out_sc[slot, :, cols])
                    + decode(p_in[slot, :, cols], p_in_sc[slot, :, cols])
                )
                d_out[slot, :, cols] = coded
                d_out_sc[slot, :, cols] = scale
                return carry

            lax.fori_loop(0, W // CB, block, 0)
            for copy in d_copies(slot):
                copy.start()

    def hand_part_in(slot):
        return (
            remote(d_out.at[slot], p_in.at[slot], p_s.at[slot], p_r.at[slot], mate),
            remote(d_out_sc.at[slot], p_in_sc.at[slot], psc_s.at[slot], psc_r.at[slot], mate),
        )

    def direct(first, last):
        count = last - first + 1

        def block(j, carry):
            part = jnp.dot(
                dense_own[first * P_DEV:(last + 1) * P_DEV, :], v_dir[:, columns(j)],
                preferred_element_type=jnp.float32,
            )
            for i in range(count):
                coded, scale = encode(part[i * P_DEV:(i + 1) * P_DEV])
                d_out[first + i, :, columns(j)] = coded
                d_out_sc[first + i, :, columns(j)] = scale
            return carry

        lax.fori_loop(0, W // CB, block, 0)

    def far_wait(slot):
        rel = REL[slot]
        fresh = shifted
        if rel in LOW_TAKES:
            fresh = fresh & jnp.logical_not(low)
        if rel in HIGH_TAKES:
            fresh = fresh & jnp.logical_not(high)

        @pl.when(fresh)
        def _():
            far_copy(slot).wait_recv()

        @pl.when(shifted)
        def _():
            expand(far, slot, dense_far)

    def mirrored(first, last):
        for slot in range(last, first - 1, -1):
            far_wait(slot)
        rows = slice(first * P_DEV, (last + 1) * P_DEV)

        def block(j, carry):
            for flag, dense in ((shifted, dense_far), (z == 0, dense_own)):
                @pl.when(flag)
                def _(dense=dense):
                    mirror[rows, columns(j)] = jnp.dot(
                        dense[rows, :], v_mir[:, columns(j)], preferred_element_type=jnp.float32
                    )
            return carry

        lax.fori_loop(0, W // CB, block, 0)

    def gathered(r):
        for piece in range(len(ROW_PIECES)):
            if r < 4 or piece < ROWS_UP:
                gather_copy(-r + 1, 1, piece).wait_recv()
            if r < 3 or (r == 3 and piece < ROWS_UP):
                gather_start(-r, 1, piece)
            if r < 4 or piece >= ROWS_UP:
                gather_copy(r - 1, -1, piece).wait_recv()
            if r < 3 or (r == 3 and piece >= ROWS_UP):
                gather_start(r, -1, piece)

    direct(7, 7)
    d_send(0)
    gathered(1)
    far_start(SLOT[-1])
    far_start(SLOT[1])
    expand(own, SLOT[-1], dense_own)
    expand(own, SLOT[1], dense_own)
    direct(5, 6)
    d_send(1)
    d_send(-1)
    far_pass(0)
    gathered(2)
    far_start(SLOT[-2])
    far_start(SLOT[2])
    expand(own, SLOT[-2], dense_own)
    expand(own, SLOT[2], dense_own)
    direct(3, 4)
    d_send(2)
    d_send(-2)
    far_pass(-1)
    far_pass(1)
    gathered(3)
    far_start(SLOT[-3])
    far_start(SLOT[3])
    expand(own, SLOT[-3], dense_own)
    expand(own, SLOT[3], dense_own)
    direct(1, 2)
    d_send(-3)
    d_send(3)
    far_pass(-2)
    far_pass(2)
    gathered(4)
    far_start(SLOT[4])
    expand(own, SLOT[4], dense_own)
    direct(0, 0)
    d_send(4)
    d_lend(4)
    mirrored(4, 7)
    far_pass(-3)
    far_pass(3)
    d_lend(3)
    d_lend(-3)
    d_lend(2)
    d_lend(-2)
    d_lend(1)
    d_lend(-1)

    def add_direct(slot):
        def add(part, part_sc):
            def block(j, carry):
                cols = columns(j)
                rows = pl.ds(slot * P_DEV, P_DEV)
                mirror[rows, cols] = mirror[rows, cols] + decode(part[slot, :, cols], part_sc[slot, :, cols])
                return carry

            lax.fori_loop(0, W // CB, block, 0)

        @pl.when(behind_sends(REL[slot]))
        def _():
            for copy in d_copies(slot):
                copy.wait_recv()
            add(d_in, d_in_sc)

        @pl.when(z == 0)
        def _():
            add(d_out, d_out_sc)

    def settle(slot, piece, lanes, last):
        def block(j, carry):
            cols = pl.ds(pl.multiple_of(piece * PW + j * B, B), B)
            total = mirror[slot * P_DEV:(slot + 1) * P_DEV, cols]
            for lane in lanes:
                total = total + decode(r_in[lane, slot, :, cols], r_in_sc[lane, slot, :, cols])
            if last:
                out_ref[:, cols] = total
            else:
                coded, scale = encode(total)
                r_out[slot, :, cols] = coded
                r_out_sc[slot, :, cols] = scale
            return carry

        lax.fori_loop(0, PW // B, block, 0)

    sum_sends = []

    def relay(far_off):
        added = set()
        for step, piece in ((1, 0), (-1, 1), (-1, 0), (1, 1)):
            begins = (step, piece) in ((1, 0), (-1, 1))
            if far_off == 4 and begins:
                continue
            rel = far_off * step
            if SLOT[rel] not in added:
                added.add(SLOT[rel])
                add_direct(SLOT[rel])
            lanes = []
            if far_off < 3 or (far_off == 3 and not begins):
                for copy in r_copies(rel + step, step, piece):
                    copy.wait_recv()
                lanes = [0 if step == 1 else 1]
            settle(SLOT[rel], piece, lanes, False)
            for copy in r_copies(rel, step, piece):
                copy.start()
                sum_sends.append(copy)

    d_merge(-2)
    d_merge(2)
    mirrored(0, 0)
    relay(4)
    d_merge(-1)
    d_merge(1)
    mirrored(1, 2)
    relay(3)
    d_merge(0)
    mirrored(3, 3)
    relay(2)
    relay(1)
    add_direct(me)
    for piece in range(COL_PIECES):
        for step in (-1, 1):
            for copy in r_copies(step, step, piece):
                copy.wait_recv()
        settle(me, piece, [0, 1], True)

    for copy in gather_sends + sum_sends:
        copy.wait_send()

    for slot, rel in enumerate(REL):
        @pl.when(behind_takes(rel))
        def _(slot=slot):
            far_copy(slot).wait_send()

        @pl.when(shifted & jnp.logical_not(lent(rel)))
        def _(slot=slot):
            for copy in d_copies(slot):
                copy.wait_send()

        for role, takes, step in ((low, LOW_TAKES, 1), (high, HIGH_TAKES, -1)):
            if rel in takes:
                @pl.when(role)
                def _(rel=rel, step=step):
                    hand_far(rel, step).wait_send()

        for role, lends, step in ((low_d, LOW_LENDS, 1), (high_d, HIGH_LENDS, -1)):
            if rel in lends:
                @pl.when(role)
                def _(rel=rel, step=step):
                    for copy in hand_part(rel, step):
                        copy.wait_send()


def shards(l_tiles, nz_lists, v_slab):
    dma = pltpu.SemaphoreType.DMA
    return pl.pallas_call(
        kernel,
        out_shape=jax.ShapeDtypeStruct((P_DEV, W), jnp.float32),
        in_specs=[
            pl.BlockSpec(memory_space=pltpu.HBM),
            pl.BlockSpec(memory_space=pltpu.HBM),
            pl.BlockSpec(memory_space=pltpu.HBM),
        ],
        out_specs=pl.BlockSpec(memory_space=pltpu.VMEM),
        scratch_shapes=[
            pltpu.SMEM((1, 1, NZ), jnp.int32),
            pltpu.VMEM((NB, MSG, B), jnp.bfloat16),
            pltpu.VMEM((NB, MSG, B), jnp.bfloat16),
            pltpu.VMEM((NB * P_DEV, W), jnp.bfloat16),
            pltpu.VMEM((NB * P_DEV, W), jnp.bfloat16),
            pltpu.VMEM((W, W), jnp.bfloat16),
            pltpu.VMEM((W, W), jnp.bfloat16),
            pltpu.VMEM((NB * P_DEV, W), jnp.float32),
            pltpu.VMEM((NB, P_DEV, W), jnp.int16),
            pltpu.VMEM((NB, 1, W), jnp.float32),
            pltpu.VMEM((NB, P_DEV, W), jnp.int16),
            pltpu.VMEM((NB, 1, W), jnp.float32),
            pltpu.VMEM((NB, P_DEV, W), jnp.int16),
            pltpu.VMEM((NB, 1, W), jnp.float32),
            pltpu.VMEM((2, NB, P_DEV, W), jnp.int16),
            pltpu.VMEM((2, NB, 1, W), jnp.float32),
            pltpu.VMEM((NB, P_DEV, W), jnp.int16),
            pltpu.VMEM((NB, 1, W), jnp.float32),
            dma((NZ + 1,)),
            dma((1,)),
            dma((NB, len(ROW_PIECES))), dma((NB, len(ROW_PIECES))),
            dma((NB,)), dma((NB,)),
            dma((NB,)), dma((NB,)), dma((NB,)), dma((NB,)),
            dma((NB, 2)), dma((2, NB, 2)), dma((NB, 2)), dma((2, NB, 2)),
            dma((NB,)), dma((NB,)), dma((NB,)), dma((NB,)), dma((NB,)),
        ],
        compiler_params=pltpu.CompilerParams(
            collective_id=0, has_side_effects=True, vmem_limit_bytes=63 << 20
        ),
    )(nz_lists, l_tiles, v_slab)


def solution(mesh):
    placed = (P("pair", "tile"), P("pair", "tile", None), P("tile", "pair", None, None))
    return jax.shard_map(
        shards, mesh=mesh, in_specs=placed, out_specs=P("pair", "tile"), check_vma=False
    )
```

```python
import functools

import jax
import jax.numpy as jnp
from jax import lax
from jax.experimental import pallas as pl
from jax.experimental.pallas import tpu as pltpu
from jax.sharding import PartitionSpec as P

MESH = pl.DeviceIdType.MESH
B = 128
KB = 10
NZ = 8
P_DEV = 96
W = B * KB
NB = 8
NG = 32
MSG = NZ * P_DEV + 16
CB = 256
ROW_PIECES = ((0, 208), (208, 192), (400, 192), (592, 192))
ROWS_UP = 2
COL_PIECES = 2
PW = W // COL_PIECES
REL = (4, -3, 3, 2, -2, 1, -1, 0)
SLOT = {rel: slot for slot, rel in enumerate(REL)}
SLOT[-4] = SLOT[4]
QMAX = 32767.0
SHARED = (2, 3, 4, 5, 6, 7)
LOW_TAKES = (0, -1, -2, -3)
LOW_GETS = (1, 2, 3, 4)
HIGH_TAKES = (0, 1, 2, 3)
HIGH_GETS = (-1, -2, -3, 4)
MERGED = (2, 3, 4, 5, 6, 7)
LOW_MERGES = (0, -1, -2)
LOW_LENDS = (1, 2, 3)


def near(rel):
    return (rel + 3) % NB - 3


HIGH_MERGES = tuple(near(rel - 1) for rel in LOW_LENDS)
HIGH_LENDS = tuple(near(rel - 1) for rel in LOW_MERGES)


def either(flags):
    return functools.reduce(jnp.logical_or, flags)


def encode(values):
    top = jnp.maximum(jnp.max(jnp.abs(values), axis=0, keepdims=True), 1e-30)
    coded = jnp.round(values * (QMAX / top)).astype(jnp.int32).astype(jnp.int16)
    return coded, top * (1.0 / QMAX)


def decode(coded, scale):
    return coded.astype(jnp.int32).astype(jnp.float32) * scale


def columns(j):
    return pl.ds(pl.multiple_of(j * CB, CB), CB)


def kernel(
    nz_ref, l_ref, v_ref, out_ref,
    lists, own, far, dense_own, dense_far, v_dir, v_mir, mirror,
    d_out, d_out_sc, d_in, d_in_sc, r_out, r_out_sc, r_in, r_in_sc, p_in, p_in_sc,
    l_sem, v_sem, ag_s, ag_r, far_s, far_r, d_s, d_r, dsc_s, dsc_r, r_s, r_r, rsc_s, rsc_r,
    fwd_s, p_s, p_r, psc_s, psc_r,
):
    t = lax.axis_index("tile")
    z = lax.axis_index("pair")
    up = (t, lax.rem(z + 1, NB))
    down = (t, lax.rem(z + NB - 1, NB))
    ahead = (lax.rem(t + z, NG), z)
    behind = (lax.rem(t + NG - z, NG), z)
    shifted = z > 0

    core = lax.rem(t, 2)
    core_behind = lax.rem(t + z, 2)
    plane_low = either([z == k - 1 for k in SHARED])
    plane_high = either([z == k for k in SHARED])
    low = (core == 1) & plane_low
    high = (core == 0) & plane_high
    mate = (t + 1 - 2 * core, z + 2 * core - 1)
    low_d = (core == 1) & either([z == k - 1 for k in MERGED])
    high_d = (core == 0) & either([z == k for k in MERGED])
    behind_low_d = (core_behind == 1) & either([z == k - 1 for k in MERGED])
    behind_high_d = (core_behind == 0) & either([z == k for k in MERGED])
    behind_low = (core_behind == 1) & plane_low
    behind_high = (core_behind == 0) & plane_high

    def behind_takes(rel):
        flag = shifted
        if rel in LOW_GETS:
            flag = flag & jnp.logical_not(behind_low)
        if rel in HIGH_GETS:
            flag = flag & jnp.logical_not(behind_high)
        return flag

    def behind_sends(rel):
        flag = shifted
        if rel in LOW_LENDS:
            flag = flag & jnp.logical_not(behind_low_d)
        if rel in HIGH_LENDS:
            flag = flag & jnp.logical_not(behind_high_d)
        return flag

    def lent(rel):
        flag = z < 0
        if rel in LOW_LENDS:
            flag = flag | low_d
        if rel in HIGH_LENDS:
            flag = flag | high_d
        return flag

    def merges(rel):
        flag = z < 0
        if rel in LOW_MERGES:
            flag = flag | low_d
        if rel in HIGH_MERGES:
            flag = flag | high_d
        return flag

    me = SLOT[0]
    list_load = pltpu.make_async_copy(nz_ref, lists, l_sem.at[NZ])
    tile_loads = [
        pltpu.make_async_copy(
            l_ref.at[:, e * B:(e + 1) * B], own.at[me, e * P_DEV:(e + 1) * P_DEV, :], l_sem.at[e]
        )
        for e in range(NZ)
    ]
    list_load.start()
    for load in tile_loads:
        load.start()
    v_load = pltpu.make_async_copy(v_ref.at[0, 0], v_dir, v_sem.at[0])
    v_load.start()

    barrier = pltpu.get_barrier_semaphore()
    for device in (up, down):
        pl.semaphore_signal(barrier, inc=1, device_id=device, device_id_type=MESH)

    @pl.when(shifted)
    def _():
        for device in (ahead, behind):
            pl.semaphore_signal(barrier, inc=1, device_id=device, device_id_type=MESH)

    @pl.when(low | high)
    def _():
        pl.semaphore_signal(barrier, inc=1, device_id=mate, device_id_type=MESH)

    list_load.wait()
    entry = lax.broadcasted_iota(jnp.int32, (16, B), 0)
    listed = jnp.zeros((16, B), jnp.int32)
    for e in range(NZ):
        listed = jnp.where(entry == e, lists[0, 0, e], listed)
    own[me, NZ * P_DEV:, :] = listed.astype(jnp.float32).astype(jnp.bfloat16)

    pl.semaphore_wait(barrier, 2 + 2 * jnp.minimum(z, 1) + (low | high).astype(jnp.int32))
    for load in tile_loads:
        load.wait()

    def remote(src, dst, send, recv, device):
        return pltpu.make_async_remote_copy(
            src_ref=src, dst_ref=dst, send_sem=send, recv_sem=recv,
            device_id=device, device_id_type=MESH,
        )

    def gather_copy(rel, step, piece):
        src, dst = SLOT[rel], SLOT[rel - step]
        rows = pl.ds(*ROW_PIECES[piece])
        return remote(
            own.at[src, rows], own.at[dst, rows], ag_s.at[dst, piece], ag_r.at[dst, piece],
            up if step == 1 else down,
        )

    def far_copy(slot):
        return remote(own.at[slot], far.at[slot], far_s.at[slot], far_r.at[slot], behind)

    def hand_far(rel, step):
        src, dst = SLOT[rel], SLOT[near(rel - step)]
        return remote(far.at[src], far.at[dst], fwd_s.at[src], far_r.at[dst], mate)

    def hand_part(rel, step):
        src, dst = SLOT[rel], SLOT[near(rel - step)]
        return (
            remote(d_out.at[src], p_in.at[dst], p_s.at[src], p_r.at[dst], mate),
            remote(d_out_sc.at[src], p_in_sc.at[dst], psc_s.at[src], psc_r.at[dst], mate),
        )

    def d_copies(slot):
        return (
            remote(d_out.at[slot], d_in.at[slot], d_s.at[slot], d_r.at[slot], ahead),
            remote(d_out_sc.at[slot], d_in_sc.at[slot], dsc_s.at[slot], dsc_r.at[slot], ahead),
        )

    def r_copies(rel, step, piece):
        src, dst = SLOT[rel], SLOT[rel - step]
        lane = 0 if step == 1 else 1
        device = up if step == 1 else down
        cols = pl.ds(piece * PW, PW)
        return (
            remote(
                r_out.at[src, :, cols], r_in.at[lane, dst, :, cols],
                r_s.at[src, piece], r_r.at[lane, dst, piece], device,
            ),
            remote(
                r_out_sc.at[src, :, cols], r_in_sc.at[lane, dst, :, cols],
                rsc_s.at[src, piece], rsc_r.at[lane, dst, piece], device,
            ),
        )

    def expand(msg, slot, dense):
        lists = msg[slot, NZ * P_DEV:, :].astype(jnp.float32)
        for k in range(KB):
            total = None
            for e in range(max(0, k - KB + NZ), min(NZ - 1, k) + 1):
                hit = jnp.where(lists[e:e + 1, :] == float(k), 1.0, 0.0).astype(jnp.bfloat16)
                term = msg[slot, e * P_DEV:(e + 1) * P_DEV, :] * hit
                total = term if total is None else total + term
            dense[slot * P_DEV:(slot + 1) * P_DEV, k * B:(k + 1) * B] = total

    gather_sends = []

    def gather_start(rel, step, piece):
        copy = gather_copy(rel, step, piece)
        copy.start()
        gather_sends.append(copy)

    def far_start(slot):
        @pl.when(behind_takes(REL[slot]))
        def _():
            far_copy(slot).start()

    def far_pass(rel):
        for role, takes, step in ((low, LOW_TAKES, 1), (high, HIGH_TAKES, -1)):
            if rel in takes:
                @pl.when(role)
                def _(step=step):
                    far_copy(SLOT[rel]).wait_recv()
                    hand_far(rel, step).start()

    for piece in range(len(ROW_PIECES)):
        gather_start(0, 1, piece)
        gather_start(0, -1, piece)
    far_start(me)
    v_load.wait()

    def turn(i, carry):
        rows = pl.ds(pl.multiple_of(i * B, B), B)

        @pl.when(shifted)
        def _():
            v_mir[:, rows] = v_dir[rows, :].T

        @pl.when(z == 0)
        def _():
            row_ids = lax.broadcasted_iota(jnp.int32, (B, W), 0) + i * B
            col_ids = lax.broadcasted_iota(jnp.int32, (B, W), 1)
            block = v_dir[rows, :].astype(jnp.float32)
            v_dir[rows, :] = jnp.where(row_ids <= col_ids, block, 0.0).astype(jnp.bfloat16)
            v_mir[:, rows] = jnp.where(row_ids < col_ids, block, 0.0).astype(jnp.bfloat16).T

        return carry

    lax.fori_loop(0, KB, turn, 0)
    expand(own, me, dense_own)

    def d_send(rel):
        slot = SLOT[rel]

        @pl.when(shifted & jnp.logical_not(lent(rel)) & jnp.logical_not(merges(rel)))
        def _():
            for copy in d_copies(slot):
                copy.start()

    def d_lend(rel):
        for role, lends, step in ((low_d, LOW_LENDS, 1), (high_d, HIGH_LENDS, -1)):
            if rel in lends:
                @pl.when(role)
                def _(step=step):
                    for copy in hand_part(rel, step):
                        copy.start()

    def d_merge(rel):
        slot = SLOT[rel]
        if rel not in LOW_MERGES + HIGH_MERGES:
            return

        @pl.when(merges(rel))
        def _():
            for copy in hand_part_in(slot):
                copy.wait_recv()

            def block(j, carry):
                cols = columns(j)
                coded, scale = encode(
                    decode(d_out[slot, :, cols], d_out_sc[slot, :, cols])
                    + decode(p_in[slot, :, cols], p_in_sc[slot, :, cols])
                )
                d_out[slot, :, cols] = coded
                d_out_sc[slot, :, cols] = scale
                return carry

            lax.fori_loop(0, W // CB, block, 0)
            for copy in d_copies(slot):
                copy.start()

    def hand_part_in(slot):
        return (
            remote(d_out.at[slot], p_in.at[slot], p_s.at[slot], p_r.at[slot], mate),
            remote(d_out_sc.at[slot], p_in_sc.at[slot], psc_s.at[slot], psc_r.at[slot], mate),
        )

    def direct(first, last):
        count = last - first + 1

        def block(j, carry):
            part = jnp.dot(
                dense_own[first * P_DEV:(last + 1) * P_DEV, :], v_dir[:, columns(j)],
                preferred_element_type=jnp.float32,
            )
            for i in range(count):
                coded, scale = encode(part[i * P_DEV:(i + 1) * P_DEV])
                d_out[first + i, :, columns(j)] = coded
                d_out_sc[first + i, :, columns(j)] = scale
            return carry

        lax.fori_loop(0, W // CB, block, 0)

    def far_wait(slot):
        rel = REL[slot]
        fresh = shifted
        if rel in LOW_TAKES:
            fresh = fresh & jnp.logical_not(low)
        if rel in HIGH_TAKES:
            fresh = fresh & jnp.logical_not(high)

        @pl.when(fresh)
        def _():
            far_copy(slot).wait_recv()

        @pl.when(shifted)
        def _():
            expand(far, slot, dense_far)

    def mirrored(first, last):
        for slot in range(last, first - 1, -1):
            far_wait(slot)
        rows = slice(first * P_DEV, (last + 1) * P_DEV)

        def block(j, carry):
            for flag, dense in ((shifted, dense_far), (z == 0, dense_own)):
                @pl.when(flag)
                def _(dense=dense):
                    mirror[rows, columns(j)] = jnp.dot(
                        dense[rows, :], v_mir[:, columns(j)], preferred_element_type=jnp.float32
                    )
            return carry

        lax.fori_loop(0, W // CB, block, 0)

    def gathered(r):
        for piece in range(len(ROW_PIECES)):
            if r < 4 or piece < ROWS_UP:
                gather_copy(-r + 1, 1, piece).wait_recv()
            if r < 3 or (r == 3 and piece < ROWS_UP):
                gather_start(-r, 1, piece)
            if r < 4 or piece >= ROWS_UP:
                gather_copy(r - 1, -1, piece).wait_recv()
            if r < 3 or (r == 3 and piece >= ROWS_UP):
                gather_start(r, -1, piece)

    direct(7, 7)
    d_send(0)
    gathered(1)
    far_start(SLOT[-1])
    far_start(SLOT[1])
    expand(own, SLOT[-1], dense_own)
    expand(own, SLOT[1], dense_own)
    direct(5, 6)
    d_send(1)
    d_send(-1)
    far_pass(0)
    gathered(2)
    far_start(SLOT[-2])
    far_start(SLOT[2])
    expand(own, SLOT[-2], dense_own)
    expand(own, SLOT[2], dense_own)
    direct(3, 4)
    d_send(2)
    d_send(-2)
    far_pass(-1)
    far_pass(1)
    gathered(3)
    far_start(SLOT[-3])
    far_start(SLOT[3])
    expand(own, SLOT[-3], dense_own)
    expand(own, SLOT[3], dense_own)
    direct(1, 2)
    d_send(-3)
    d_send(3)
    far_pass(-2)
    far_pass(2)
    gathered(4)
    far_start(SLOT[4])
    expand(own, SLOT[4], dense_own)
    direct(0, 0)
    d_send(4)
    d_lend(4)
    mirrored(4, 7)
    far_pass(-3)
    far_pass(3)
    d_lend(3)
    d_lend(-3)
    d_lend(2)
    d_lend(-2)
    d_lend(1)
    d_lend(-1)

    def add_direct(slot):
        def add(part, part_sc):
            def block(j, carry):
                cols = columns(j)
                rows = pl.ds(slot * P_DEV, P_DEV)
                mirror[rows, cols] = mirror[rows, cols] + decode(part[slot, :, cols], part_sc[slot, :, cols])
                return carry

            lax.fori_loop(0, W // CB, block, 0)

        @pl.when(behind_sends(REL[slot]))
        def _():
            for copy in d_copies(slot):
                copy.wait_recv()
            add(d_in, d_in_sc)

        @pl.when(z == 0)
        def _():
            add(d_out, d_out_sc)

    def settle(slot, piece, lanes, last):
        def block(j, carry):
            cols = pl.ds(pl.multiple_of(piece * PW + j * B, B), B)
            total = mirror[slot * P_DEV:(slot + 1) * P_DEV, cols]
            for lane in lanes:
                total = total + decode(r_in[lane, slot, :, cols], r_in_sc[lane, slot, :, cols])
            if last:
                out_ref[:, cols] = total
            else:
                coded, scale = encode(total)
                r_out[slot, :, cols] = coded
                r_out_sc[slot, :, cols] = scale
            return carry

        lax.fori_loop(0, PW // B, block, 0)

    sum_sends = []

    def relay(far_off):
        added = set()
        for step, piece in ((1, 0), (-1, 1), (-1, 0), (1, 1)):
            begins = (step, piece) in ((1, 0), (-1, 1))
            if far_off == 4 and begins:
                continue
            rel = far_off * step
            if SLOT[rel] not in added:
                added.add(SLOT[rel])
                add_direct(SLOT[rel])
            lanes = []
            if far_off < 3 or (far_off == 3 and not begins):
                for copy in r_copies(rel + step, step, piece):
                    copy.wait_recv()
                lanes = [0 if step == 1 else 1]
            settle(SLOT[rel], piece, lanes, False)
            for copy in r_copies(rel, step, piece):
                copy.start()
                sum_sends.append(copy)

    mirrored(0, 0)
    relay(4)
    d_merge(-2)
    d_merge(2)
    d_merge(-1)
    d_merge(1)
    mirrored(1, 2)
    relay(3)
    d_merge(0)
    mirrored(3, 3)
    relay(2)
    relay(1)
    add_direct(me)
    for piece in range(COL_PIECES):
        for step in (-1, 1):
            for copy in r_copies(step, step, piece):
                copy.wait_recv()
        settle(me, piece, [0, 1], True)

    for copy in gather_sends + sum_sends:
        copy.wait_send()

    for slot, rel in enumerate(REL):
        @pl.when(behind_takes(rel))
        def _(slot=slot):
            far_copy(slot).wait_send()

        @pl.when(shifted & jnp.logical_not(lent(rel)))
        def _(slot=slot):
            for copy in d_copies(slot):
                copy.wait_send()

        for role, takes, step in ((low, LOW_TAKES, 1), (high, HIGH_TAKES, -1)):
            if rel in takes:
                @pl.when(role)
                def _(rel=rel, step=step):
                    hand_far(rel, step).wait_send()

        for role, lends, step in ((low_d, LOW_LENDS, 1), (high_d, HIGH_LENDS, -1)):
            if rel in lends:
                @pl.when(role)
                def _(rel=rel, step=step):
                    for copy in hand_part(rel, step):
                        copy.wait_send()


def shards(l_tiles, nz_lists, v_slab):
    dma = pltpu.SemaphoreType.DMA
    return pl.pallas_call(
        kernel,
        out_shape=jax.ShapeDtypeStruct((P_DEV, W), jnp.float32),
        in_specs=[
            pl.BlockSpec(memory_space=pltpu.HBM),
            pl.BlockSpec(memory_space=pltpu.HBM),
            pl.BlockSpec(memory_space=pltpu.HBM),
        ],
        out_specs=pl.BlockSpec(memory_space=pltpu.VMEM),
        scratch_shapes=[
            pltpu.SMEM((1, 1, NZ), jnp.int32),
            pltpu.VMEM((NB, MSG, B), jnp.bfloat16),
            pltpu.VMEM((NB, MSG, B), jnp.bfloat16),
            pltpu.VMEM((NB * P_DEV, W), jnp.bfloat16),
            pltpu.VMEM((NB * P_DEV, W), jnp.bfloat16),
            pltpu.VMEM((W, W), jnp.bfloat16),
            pltpu.VMEM((W, W), jnp.bfloat16),
            pltpu.VMEM((NB * P_DEV, W), jnp.float32),
            pltpu.VMEM((NB, P_DEV, W), jnp.int16),
            pltpu.VMEM((NB, 1, W), jnp.float32),
            pltpu.VMEM((NB, P_DEV, W), jnp.int16),
            pltpu.VMEM((NB, 1, W), jnp.float32),
            pltpu.VMEM((NB, P_DEV, W), jnp.int16),
            pltpu.VMEM((NB, 1, W), jnp.float32),
            pltpu.VMEM((2, NB, P_DEV, W), jnp.int16),
            pltpu.VMEM((2, NB, 1, W), jnp.float32),
            pltpu.VMEM((NB, P_DEV, W), jnp.int16),
            pltpu.VMEM((NB, 1, W), jnp.float32),
            dma((NZ + 1,)),
            dma((1,)),
            dma((NB, len(ROW_PIECES))), dma((NB, len(ROW_PIECES))),
            dma((NB,)), dma((NB,)),
            dma((NB,)), dma((NB,)), dma((NB,)), dma((NB,)),
            dma((NB, 2)), dma((2, NB, 2)), dma((NB, 2)), dma((2, NB, 2)),
            dma((NB,)), dma((NB,)), dma((NB,)), dma((NB,)), dma((NB,)),
        ],
        compiler_params=pltpu.CompilerParams(
            collective_id=0, has_side_effects=True, vmem_limit_bytes=63 << 20
        ),
    )(nz_lists, l_tiles, v_slab)


def solution(mesh):
    placed = (P("pair", "tile"), P("pair", "tile", None), P("tile", "pair", None, None))
    return jax.shard_map(
        shards, mesh=mesh, in_specs=placed, out_specs=P("pair", "tile"), check_vma=False
    )
```
